32 devices in a mesh: worker: 1, fsdp: 32 (over z, y, x, core).
Axes of the slice: x: 2, y: 2, z: 4, core: 2. Of those that a mesh axis runs over, the one named last changes fastest.
Arguments:
- inputs: bfloat16 [1, 2, 4096, 8192], P('worker', None, 'fsdp'), may hold values from -6 to 6
- targets: bfloat16 [1, 2, 4096, 512], P('worker', None, 'fsdp'), may hold values from -6 to 6
- base: float32 [8192, 512], P('fsdp', 'worker'), may hold values from -6 to 6
- adapter_a: float32 [1, 64, 8192], P('worker', None, 'fsdp'), may hold values from -6 to 6
- adapter_b: float32 [1, 512, 64], P('worker'), may hold values from -3 to 3
Outputs:
- new_base: float32 [8192, 512], P('fsdp', 'worker')
- final_a: float32 [1, 64, 8192], P('worker', None, 'fsdp')
- final_b: float32 [1, 512, 64], P('worker')
The draws below stay inside these ranges and needn't reach their ends.
All inputs are finite; a program needn't handle non-finite values.
Results may differ from the reference program's by a relative error of at most 0.0048.
Values may be sent and summed in bfloat16 or wider, within the bound.
A program may use at most 64 MiB of HBM per device.

```python
import jax
import jax.numpy as jnp
from jax import lax

D = 8192
KW = 512
R = 64
STEPS = 2
TOKENS = 4096
WORKERS = 1


def spiked(array, rng, source, target, parts, factor):
    def block_of(axis_at):
        return (jnp.arange(array.shape[axis_at]) // (array.shape[axis_at] // parts)).reshape((-1,) + (1,) * (array.ndim - 1 - axis_at))

    near = jax.random.permutation(rng, parts)[block_of(target)]
    other_side = (block_of(target) + parts // 2) % parts
    return jnp.where((block_of(source) == near) | (block_of(source) == other_side), factor * array, array)


def block_scale(stream_key, extent, shards, smallest, largest):
    def one(axis_at, blocks):
        heights = jax.random.uniform(jax.random.fold_in(jax.random.fold_in(stream_key, 6), axis_at), (blocks,), jnp.float32, smallest / len(shards), largest / len(shards))
        return jnp.repeat(jnp.exp(heights), extent[axis_at] // blocks).reshape((-1,) + (1,) * (len(extent) - axis_at - 1))

    loudness = one(*shards[0])
    for cut in shards[1:]:
        loudness = loudness * one(*cut)
    return loudness


def noise(key, dims, deviation, most, split=(), kind=jnp.bfloat16):
    drawn = jax.random.normal(key, dims, jnp.float32) * deviation
    if len(split) > 0:
        drawn = block_scale(key, dims, split, -0.22, 0.18) * drawn
    return jnp.clip(drawn, min=-most, max=most).astype(kind)


def heavy_noise(key, extent, deviation, limit, pieces, heavy, dtype=jnp.bfloat16):
    entries = deviation * jax.random.normal(key, extent, jnp.float32)
    if pieces:
        entries = entries * block_scale(key, extent, pieces, -0.22, 0.18)
    return jnp.clip(spiked(entries, jax.random.fold_in(key, 3), *heavy), -limit, limit).astype(dtype)


def setup_inputs(seed: int = 0) -> dict:
    keys = jax.random.split(jax.random.key(seed), 6)
    return {
        "inputs": heavy_noise(keys[0], (WORKERS, STEPS, TOKENS, D), 1.0, 6.0, ((2, 32),), (2, 3, 32, 2.75)),
        "targets": noise(keys[1], (WORKERS, STEPS, TOKENS, KW), 1.0, 6.0, ((2, 32),)),
        "base": noise(keys[2], (D, KW), 1.0, 6.0, ((0, 32),), jnp.float32),
        "adapter_a": noise(keys[3], (WORKERS, R, D), 1.0, 6.0, ((2, 32),), jnp.float32),
        "adapter_b": noise(keys[4], (WORKERS, KW, R), 0.5, 3.0, (), jnp.float32),
    }


branch_scale = 0.25
rate_down = 200.0
rate_up = 20.0


def reference(inputs, targets, base, adapter_a, adapter_b):
    high = lax.Precision.HIGHEST
    scale = D ** -0.5
    base_half = base.astype(jnp.bfloat16)

    def train_worker(total, pack):
        tokens, wanted, a_start, b_start = pack
        adapter, upper = a_start, b_start
        for step in range(STEPS):
            keys_base = jnp.dot(tokens[step], base_half, preferred_element_type=jnp.float32) * scale
            a_half = adapter.astype(jnp.bfloat16)
            low = jnp.dot(tokens[step], a_half.T, preferred_element_type=jnp.float32) * scale
            output = keys_base + branch_scale * jnp.dot(low, upper.T, precision=high)
            error = (output - wanted[step].astype(jnp.float32)) / TOKENS
            grad_b = branch_scale * jnp.dot(error.T, low, precision=high)
            back = (branch_scale * jnp.dot(error, upper, precision=high)).astype(jnp.bfloat16)
            grad_a = jnp.dot(back.T, tokens[step], preferred_element_type=jnp.float32) * scale
            adapter = adapter - rate_down * grad_a
            upper = upper - rate_up * grad_b
        change = branch_scale * (jnp.dot(adapter.T, upper.T, precision=high) - jnp.dot(a_start.T, b_start.T, precision=high))
        return total + change, (adapter, upper)

    total, finals = lax.scan(train_worker, jnp.zeros(base.shape, jnp.float32), (inputs, targets, adapter_a, adapter_b))
    new_base = base + total / WORKERS
    return new_base, finals[0], finals[1]
```

```python
import functools
import itertools

import jax
import jax.numpy as jnp
from jax import lax
from jax.experimental import pallas as pl
from jax.experimental.pallas import tpu as pltpu
from jax.sharding import PartitionSpec as P

branch_scale = 0.25
rate_down = 200.0
rate_up = 20.0
MESH = pl.DeviceIdType.MESH
f32 = jnp.float32
bf16 = jnp.bfloat16


def nn(a, b):
    return jnp.dot(a, b, preferred_element_type=f32)


def nt(a, b):
    return lax.dot_general(a, b, (((1,), (1,)), ((), ())), preferred_element_type=f32)


def exact(a, b, dims):
    return lax.dot_general(a, b, (dims, ((), ())), precision=lax.Precision.HIGHEST, preferred_element_type=f32)


def split(a):
    high = a.astype(bf16)
    return high, (a - high.astype(f32)).astype(bf16)


def together(*tasks):
    results = [None] * len(tasks)
    live = dict(enumerate(tasks))
    while live:
        for i in list(live):
            try:
                next(live[i])
            except StopIteration as stop:
                results[i] = stop.value
                del live[i]
    return results


def kernel(
    nz, add_base, x_hbm, y_ref, base_ref, a_ref, b_ref,
    nb_ref, fa_ref, fb_ref,
    x, g, keep, send_c, recv_c, send_xy, recv_xy, send_z, recv_z,
    ar, ar_c, ar_xy, ar_z, ar_fin, send_sem, recv_sem, local_sem,
):
    me = lax.axis_index("fsdp")
    c, q, z = me % 2, (me // 2) % 4, me // 8
    qx, qy = q % 2, q // 2
    steps, rows, width = x.shape
    rank, shard = a_ref.shape
    scale = width ** (-0.5)
    total_rows = float(rows * 8 * nz)

    def device(zz, qq, cc):
        return {"fsdp": (zz * 4 + qq) * 2 + cc}

    def near(m):
        return (1 - qy if m & 2 else qy) * 2 + (1 - qx if m & 1 else qx)

    def up(k):
        return (z + k) % nz

    def down(k):
        return (z + nz - k) % nz

    core_peer = device(z, q, 1 - c)
    serial = itertools.count()
    sent = []

    def send(src, dst, peer, lands):
        i = next(serial)
        copy = pltpu.make_async_remote_copy(
            src_ref=src, dst_ref=dst, send_sem=send_sem.at[i], recv_sem=recv_sem.at[i],
            device_id=peer, device_id_type=MESH,
        )
        copy.start()
        sent.append(copy)
        return pltpu.make_async_remote_copy(
            src_ref=lands, dst_ref=lands, send_sem=send_sem.at[i], recv_sem=recv_sem.at[i],
            device_id=peer, device_id_type=MESH,
        )

    loads = [pltpu.make_async_copy(x_hbm.at[j], x.at[j], local_sem.at[j]) for j in range(steps)]
    for load in loads:
        load.start()

    barrier = pltpu.get_barrier_semaphore()
    peers = [core_peer] + [device(z, near(m), c) for m in (1, 2, 3)] + [device(up(k), q, c) for k in range(1, nz)]
    for peer in peers:
        pl.semaphore_signal(barrier, inc=1, device_id=peer, device_id_type=MESH)

    half = base_ref[...].astype(bf16)
    a_now = a_ref[...]
    b_now = b_ref[...]

    def lifted(b):
        high, low = split(b)
        return (nt(high, half) + nt(low, half)).astype(bf16)

    g[0, c, q, z, 0] = a_now.astype(bf16)
    g[0, c, q, z, 1] = lifted(b_now)
    pl.semaphore_wait(barrier, len(peers))

    def gather(step, first, count):
        part = pl.ds(first, count)

        def block(cc, qq, zz):
            return g.at[step, cc, qq, zz, part]

        def line(cc, qq):
            return g.at[step, cc, qq, :, part]

        from_z = [
            send(block(c, q, z), block(c, q, z), device(up(k), q, c), block(c, q, down(k))) for k in range(1, nz)
        ]
        from_xy = {m: [] for m in (1, 2, 3)}
        for k in range(nz):
            if k:
                yield
                from_z[k - 1].wait_recv()
            for m in (1, 2, 3):
                from_xy[m].append(
                    send(block(c, q, down(k)), block(c, q, down(k)), device(z, near(m), c), block(c, near(m), down(k)))
                )
        from_core = [send(line(c, q), line(c, q), core_peer, line(1 - c, q))]
        for m in (1, 2, 3):
            yield
            for arrival in from_xy[m]:
                arrival.wait_recv()
            from_core.append(send(line(c, near(m)), line(c, near(m)), core_peer, line(1 - c, near(m))))
        for arrival in from_core:
            yield
            arrival.wait_recv()

    def project(step, first, count):
        def body(i, total):
            for j in range(8):
                block = g[step, j % 2, j // 2, i, pl.ds(first, count)].reshape(count * rank, shard)
                columns = pl.ds(pl.multiple_of((i * 8 + j) * shard, shard), shard)
                total = total + nt(block, x[step, :, columns])
            return total

        return scale * lax.fori_loop(0, nz, body, jnp.zeros((count * rank, rows), f32))

    def scatter(step, part, left):
        def product(cc, qq, zz):
            d = (zz * 4 + qq) * 2 + cc
            return nn(left, x[step, :, pl.ds(pl.multiple_of(d * shard, shard), shard)])

        from_core = {}
        for m in (1, 2, 3, 0):
            for zz in range(nz):
                send_c[step, part, m, zz] = product(1 - c, near(m), zz).astype(bf16)
            spot = recv_c.at[step, part, m]
            from_core[m] = send(send_c.at[step, part, m], spot, core_peer, spot)
        for m in (1, 2, 3, 0):
            for zz in range(nz):
                keep[part, m, zz] = product(c, near(m), zz)
        yield
        from_xy = []
        for m in (1, 2, 3):
            from_core[m].wait_recv()
            send_xy[step, part, m - 1] = (keep[part, m] + recv_c[step, part, m].astype(f32)).astype(bf16)
            spot = recv_xy.at[step, part, m - 1]
            from_xy.append(send(send_xy.at[step, part, m - 1], spot, device(z, near(m), c), spot))
        from_core[0].wait_recv()
        yield
        for arrival in from_xy:
            arrival.wait_recv()

        def held(zz):
            value = keep[part, 0, zz] + recv_c[step, part, 0, zz].astype(f32)
            for m in (0, 1, 2):
                value = value + recv_xy[step, part, m, zz].astype(f32)
            return value

        from_z = []
        for k in range(1, nz):
            send_z[step, part, k - 1] = held(up(k)).astype(bf16)
            spot = recv_z.at[step, part, k - 1]
            from_z.append(send(send_z.at[step, part, k - 1], spot, device(up(k), q, c), spot))
        value = held(z)
        yield
        for k, arrival in enumerate(from_z):
            arrival.wait_recv()
            value = value + recv_z[step, part, k].astype(f32)
        return value

    def reduce(step, value):
        cut = rank // 2
        ar[step, 0] = value[:cut]
        ar[step, 1] = value[cut:]
        arrival = send(ar.at[step, 1 - c], ar_c.at[step], core_peer, ar_c.at[step])
        yield
        arrival.wait_recv()
        ar_xy[step, q] = (ar[step, c] + ar_c[step]).astype(bf16)
        arrivals = [
            send(ar_xy.at[step, q], ar_xy.at[step, q], device(z, near(m), c), ar_xy.at[step, near(m)])
            for m in (1, 2, 3)
        ]
        yield
        for arrival in arrivals:
            arrival.wait_recv()
        value = ar_xy[step, 0].astype(f32)
        for i in range(1, 4):
            value = value + ar_xy[step, i].astype(f32)
        ar_z[step, z] = value.astype(bf16)
        arrivals = [
            send(ar_z.at[step, z], ar_z.at[step, z], device(up(k), q, c), ar_z.at[step, down(k)])
            for k in range(1, nz)
        ]
        yield
        for arrival in arrivals:
            arrival.wait_recv()
        value = ar_z[step, 0].astype(f32)
        for i in range(1, nz):
            value = value + ar_z[step, i].astype(f32)
        ar_fin[step, c] = value
        arrival = send(ar_fin.at[step, c], ar_fin.at[step, c], core_peer, ar_fin.at[step, 1 - c])
        yield
        arrival.wait_recv()
        return jnp.concatenate([ar_fin[step, 0], ar_fin[step, 1]], axis=0)

    def back_of(step, low, lift, b):
        high, rest = split(b)
        wanted = nt(high, y_ref[step]) + nt(rest, y_ref[step])
        branch = exact(exact(b, b, ((1,), (1,))), low, ((1,), (0,)))
        return ((branch_scale / total_rows) * (lift + branch_scale * branch - wanted)).astype(bf16)

    def up_part(step, low, low_half, spread, b):
        high, rest = split(spread)
        keys = scale * (nn(high, half) + nn(rest, half))
        gram = exact(low_half.astype(f32), low, ((1,), (1,)))
        branch = branch_scale * exact(gram, b, ((1,), (0,)))
        return (branch_scale / total_rows) * (keys + branch - nn(low_half, y_ref[step]))

    state = {"b": b_now, "a": a_now}

    def up_chain(step, low, low_half):
        spread = yield from scatter(step, 0, low_half)
        value = up_part(step, low, low_half, spread, state["b"])
        grad = yield from reduce(step, value)
        state["b"] = state["b"] - rate_up * grad

    def down_chain(step, back):
        grad = yield from scatter(step, 1, back)
        state["a"] = state["a"] - (rate_down * scale) * grad

    together(gather(0, 0, 2))
    for load in loads:
        load.wait()
    both = project(0, 0, 2)
    low, lift = both[:rank], both[rank:]
    low_half = low.astype(bf16)
    back = back_of(0, low, lift, b_now)

    for step in range(steps):
        last = step + 1 == steps

        def first(step=step, low=low, low_half=low_half, last=last):
            yield from up_chain(step, low, low_half)
            if not last:
                g[step + 1, c, q, z, 1] = lifted(state["b"])
                yield from gather(step + 1, 1, 1)

        def second(step=step, back=back, last=last):
            yield from down_chain(step, back)
            if not last:
                g[step + 1, c, q, z, 0] = state["a"].astype(bf16)
                yield from gather(step + 1, 0, 1)
                return project(step + 1, 0, 1)

        _, low = together(first(), second())
        if not last:
            low_half = low.astype(bf16)
            back = back_of(step + 1, low, project(step + 1, 1, 1), state["b"])

    fa_ref[...] = state["a"]
    fb_ref[...] = state["b"]
    left = jnp.concatenate([state["a"], -a_now], axis=0).T
    right = jnp.concatenate([state["b"], b_now], axis=0)
    change = branch_scale * exact(left, right, ((1,), (0,)))
    nb_ref[...] = base_ref[...] + change if add_base else change
    for copy in sent:
        copy.wait_send()


def local(inputs, targets, base, adapter_a, adapter_b):
    n = lax.axis_size("fsdp")
    workers = lax.axis_size("worker")
    nz = n // 8
    tokens, wanted, a, b = inputs[0], targets[0], adapter_a[0], adapter_b[0].T
    steps, rows, width = tokens.shape
    rank, shard = a.shape
    features = b.shape[1]
    whole = base
    if workers > 1:
        whole = lax.all_gather(base.astype(bf16), "worker", axis=1, tiled=True).astype(f32)
    vmem = pl.BlockSpec(memory_space=pltpu.VMEM)
    block = (rank, shard)
    cut = (rank // 2, features)
    nzs = max(nz - 1, 1)
    per_gather = (nz - 1) + 3 * nz + 4
    messages = (2 * steps - 1) * per_gather + 2 * steps * (7 + nz - 1) + steps * (5 + nz - 1)
    merged, final_a, final_b = pl.pallas_call(
        functools.partial(kernel, nz, workers == 1),
        out_shape=(
            jax.ShapeDtypeStruct((shard, features), f32),
            jax.ShapeDtypeStruct(block, f32),
            jax.ShapeDtypeStruct((rank, features), f32),
        ),
        in_specs=[pl.BlockSpec(memory_space=pl.ANY)] + [vmem] * 4,
        out_specs=(vmem, vmem, vmem),
        scratch_shapes=[
            pltpu.VMEM((steps, rows, width), bf16),
            pltpu.VMEM((steps, 2, 4, nz, 2) + block, bf16),
            pltpu.VMEM((2, 4, nz) + block, f32),
            pltpu.VMEM((steps, 2, 4, nz) + block, bf16),
            pltpu.VMEM((steps, 2, 4, nz) + block, bf16),
            pltpu.VMEM((steps, 2, 3, nz) + block, bf16),
            pltpu.VMEM((steps, 2, 3, nz) + block, bf16),
            pltpu.VMEM((steps, 2, nzs) + block, bf16),
            pltpu.VMEM((steps, 2, nzs) + block, bf16),
            pltpu.VMEM((steps, 2) + cut, f32),
            pltpu.VMEM((steps,) + cut, f32),
            pltpu.VMEM((steps, 4) + cut, bf16),
            pltpu.VMEM((steps, nz) + cut, bf16),
            pltpu.VMEM((steps, 2) + cut, f32),
            pltpu.SemaphoreType.DMA((messages,)),
            pltpu.SemaphoreType.DMA((messages,)),
            pltpu.SemaphoreType.DMA((steps,)),
        ],
        compiler_params=pltpu.CompilerParams(
            collective_id=0, has_side_effects=True, vmem_limit_bytes=48 * 1024 * 1024
        ),
    )(tokens, wanted, whole, a, b)
    if workers > 1:
        share = lax.psum_scatter(merged, "worker", scatter_dimension=1, tiled=True)
        merged = base + share / workers
    return (merged, final_a[None], final_b.T[None])


def solution(mesh):
    return jax.shard_map(
        local,
        mesh=mesh,
        in_specs=(
            P("worker", None, "fsdp", None),
            P("worker", None, "fsdp", None),
            P("fsdp", "worker"),
            P("worker", None, "fsdp"),
            P("worker", None, None),
        ),
        out_specs=(P("fsdp", "worker"), P("worker", None, "fsdp"), P("worker", None, None)),
        check_vma=False,
    )
```

```python
import functools
import itertools

import jax
import jax.numpy as jnp
from jax import lax
from jax.experimental import pallas as pl
from jax.experimental.pallas import tpu as pltpu
from jax.sharding import PartitionSpec as P

branch_scale = 0.25
rate_down = 200.0
rate_up = 20.0
MESH = pl.DeviceIdType.MESH
ORDER = "0101001"
f32 = jnp.float32
bf16 = jnp.bfloat16


def nn(a, b):
    return jnp.dot(a, b, preferred_element_type=f32)


def nt(a, b):
    return lax.dot_general(a, b, (((1,), (1,)), ((), ())), preferred_element_type=f32)


def exact(a, b, dims):
    return lax.dot_general(a, b, (dims, ((), ())), precision=lax.Precision.HIGHEST, preferred_element_type=f32)


def split(a):
    high = a.astype(bf16)
    return high, (a - high.astype(f32)).astype(bf16)


def together(tasks, order=""):
    live = dict(enumerate(tasks))
    turns = [int(turn) for turn in order]
    while live:
        for i in turns or list(live):
            if i in live and next(live[i], True):
                del live[i]
        turns = []


def kernel(
    nz, add_base, x_hbm, y_hbm, base_hbm, a_hbm, b_hbm,
    nb_ref, fa_ref, fb_ref,
    x, y_ref, base_ref, a_ref, b_ref, g, keep, send_c, recv_c, send_xy, recv_xy, send_z, recv_z,
    ar, ar_in, ar_z, ar_fin, send_sem, recv_sem, local_sem,
):
    me = lax.axis_index("fsdp")
    c, q, z = me % 2, (me // 2) % 4, me // 8
    qx, qy = q % 2, q // 2
    steps, rows, width = x.shape
    rank, shard = a_ref.shape
    scale = width ** (-0.5)
    total_rows = float(rows * 8 * nz)

    def device(zz, qq, cc):
        return {"fsdp": (zz * 4 + qq) * 2 + cc}

    def near(m):
        return (1 - qy if m & 2 else qy) * 2 + (1 - qx if m & 1 else qx)

    def up(k):
        return (z + k) % nz

    def down(k):
        return (z + nz - k) % nz

    core_peer = device(z, q, 1 - c)
    serial = itertools.count()
    sent = []

    def send(src, dst, peer, lands):
        i = next(serial)
        copy = pltpu.make_async_remote_copy(
            src_ref=src, dst_ref=dst, send_sem=send_sem.at[i], recv_sem=recv_sem.at[i],
            device_id=peer, device_id_type=MESH,
        )
        copy.start()
        sent.append(copy)
        return pltpu.make_async_remote_copy(
            src_ref=lands, dst_ref=lands, send_sem=send_sem.at[i], recv_sem=recv_sem.at[i],
            device_id=peer, device_id_type=MESH,
        )

    pairs = [(base_hbm, base_ref), (b_hbm, b_ref), (a_hbm, a_ref)]
    pairs += [(x_hbm.at[j], x.at[j]) for j in range(steps)] + [(y_hbm, y_ref)]
    loads = [pltpu.make_async_copy(src, dst, local_sem.at[j]) for j, (src, dst) in enumerate(pairs)]
    for load in loads:
        load.start()

    barrier = pltpu.get_barrier_semaphore()
    cell = [(m, flip) for flip in (0, 1) for m in range(4)][1:]

    def member(m, flip):
        return near(m), 1 - c if flip else c

    peers = [device(z, *member(m, flip)) for m, flip in cell] + [device(up(k), q, c) for k in range(1, nz)]
    for peer in peers:
        pl.semaphore_signal(barrier, inc=1, device_id=peer, device_id_type=MESH)

    for load in loads[:3]:
        load.wait()
    half = base_ref[...].astype(bf16)
    a_now = a_ref[...]
    b_now = b_ref[...]

    def lifted(b):
        high, low = split(b)
        return (nt(high, half) + nt(low, half)).astype(bf16)

    g[0, c, q, z, 0] = a_now.astype(bf16)
    g[0, c, q, z, 1] = lifted(b_now)
    pl.semaphore_wait(barrier, len(peers))

    def gather(step, first, count):
        part = pl.ds(first, count)

        def block(cc, qq, zz):
            return g.at[step, cc, qq, zz, part]

        def line(cc, qq):
            return g.at[step, cc, qq, :, part]

        from_z = [
            send(block(c, q, z), block(c, q, z), device(up(k), q, c), block(c, q, down(k))) for k in range(1, nz)
        ]
        from_xy = {m: [] for m in (1, 2, 3)}
        for k in range(nz):
            if k:
                yield
                from_z[k - 1].wait_recv()
            for m in (1, 2, 3):
                from_xy[m].append(
                    send(block(c, q, down(k)), block(c, q, down(k)), device(z, near(m), c), block(c, near(m), down(k)))
                )
        from_core = [send(line(c, q), line(c, q), core_peer, line(1 - c, q))]
        for m in (1, 2, 3):
            yield
            for arrival in from_xy[m]:
                arrival.wait_recv()
            from_core.append(send(line(c, near(m)), line(c, near(m)), core_peer, line(1 - c, near(m))))
        for arrival in from_core:
            yield
            arrival.wait_recv()

    def project(step, first, count):
        def body(i, total):
            for j in range(8):
                block = g[step, j % 2, j // 2, i, pl.ds(first, count)].reshape(count * rank, shard)
                columns = pl.ds(pl.multiple_of((i * 8 + j) * shard, shard), shard)
                total = total + nt(block, x[step, :, columns])
            return total

        return scale * lax.fori_loop(0, nz, body, jnp.zeros((count * rank, rows), f32))

    def scatter(step, part, left):
        def product(cc, qq, zz):
            d = (zz * 4 + qq) * 2 + cc
            return nn(left, x[step, :, pl.ds(pl.multiple_of(d * shard, shard), shard)])

        from_core = {}
        for m in (1, 2, 3, 0):
            for zz in range(nz):
                send_c[step, part, m, zz] = product(1 - c, near(m), zz).astype(bf16)
            spot = recv_c.at[step, part, m]
            from_core[m] = send(send_c.at[step, part, m], spot, core_peer, spot)
        for m in (1, 2, 3, 0):
            for zz in range(nz):
                keep[part, m, zz] = product(c, near(m), zz)
        yield
        from_xy = []
        for m in (1, 2, 3):
            from_core[m].wait_recv()
            send_xy[step, part, m - 1] = (keep[part, m] + recv_c[step, part, m].astype(f32)).astype(bf16)
            spot = recv_xy.at[step, part, m - 1]
            from_xy.append(send(send_xy.at[step, part, m - 1], spot, device(z, near(m), c), spot))
        from_core[0].wait_recv()
        yield
        for arrival in from_xy:
            arrival.wait_recv()

        def held(zz):
            value = keep[part, 0, zz] + recv_c[step, part, 0, zz].astype(f32)
            for m in (0, 1, 2):
                value = value + recv_xy[step, part, m, zz].astype(f32)
            return value

        from_z = []
        for k in range(1, nz):
            send_z[step, part, k - 1] = held(up(k)).astype(bf16)
            spot = recv_z.at[step, part, k - 1]
            from_z.append(send(send_z.at[step, part, k - 1], spot, device(up(k), q, c), spot))
        value = held(z)
        yield
        for k, arrival in enumerate(from_z):
            arrival.wait_recv()
            value = value + recv_z[step, part, k].astype(f32)
        return value

    def reduce(step, value):
        ar[step] = value.reshape(ar.shape[1:])
        place = q * 2 + c
        arrivals = []
        for i, (m, flip) in enumerate(cell):
            qq, cc = member(m, flip)
            spot = ar_in.at[step, i]
            arrivals.append(send(ar.at[step, qq * 2 + cc], spot, device(z, qq, cc), spot))
        yield
        value = ar[step, place]
        for i, arrival in enumerate(arrivals):
            arrival.wait_recv()
            value = value + ar_in[step, i]
        ar_z[step, z] = value
        arrivals = [
            send(ar_z.at[step, z], ar_z.at[step, z], device(up(k), q, c), ar_z.at[step, down(k)])
            for k in range(1, nz)
        ]
        yield
        for arrival in arrivals:
            arrival.wait_recv()
        value = ar_z[step, 0]
        for i in range(1, nz):
            value = value + ar_z[step, i]
        ar_fin[step, place] = value
        arrivals = []
        for m, flip in cell:
            qq, cc = member(m, flip)
            own = ar_fin.at[step, place]
            arrivals.append(send(own, own, device(z, qq, cc), ar_fin.at[step, qq * 2 + cc]))
        yield
        for arrival in arrivals:
            arrival.wait_recv()
        return ar_fin[step].reshape(rank, -1)

    def back_of(step, low, lift, b):
        high, rest = split(b)
        wanted = nt(high, y_ref[step]) + nt(rest, y_ref[step])
        branch = exact(exact(b, b, ((1,), (1,))), low, ((1,), (0,)))
        return ((branch_scale / total_rows) * (lift + branch_scale * branch - wanted)).astype(bf16)

    def up_part(step, low, low_half, spread, b):
        high, rest = split(spread)
        keys = scale * (nn(high, half) + nn(rest, half))
        gram = exact(low_half.astype(f32), low, ((1,), (1,)))
        branch = branch_scale * exact(gram, b, ((1,), (0,)))
        return (branch_scale / total_rows) * (keys + branch - nn(low_half, y_ref[step]))

    state = {("b", 0): b_now, ("a", 0): a_now}

    def ready(*key):
        while key not in state:
            yield

    def up_chain(step):
        yield from ready("low", step)
        low = state["low", step]
        low_half = low.astype(bf16)
        spread = yield from scatter(step, 0, low_half)
        yield from ready("b", step)
        b = state["b", step]
        grad = yield from reduce(step, up_part(step, low, low_half, spread, b))
        state["b", step + 1] = b - rate_up * grad

    def lift_chain(step):
        g[step, c, q, z, 1] = lifted(state["b", step])
        yield from gather(step, 1, 1)
        state["lift", step] = project(step, 1, 1)

    def down_chain(step):
        yield from ready("lift", step)
        yield from ready("low", step)
        back = back_of(step, state["low", step], state["lift", step], state["b", step])
        grad = yield from scatter(step, 1, back)
        state["a", step + 1] = state["a", step] - (rate_down * scale) * grad

    def low_chain(step):
        g[step, c, q, z, 0] = state["a", step].astype(bf16)
        yield from gather(step, 0, 1)
        state["low", step] = project(step, 0, 1)

    def first():
        for step in range(0, steps, 2):
            yield from up_chain(step)
            if step + 1 < steps:
                yield from lift_chain(step + 1)
                yield from down_chain(step + 1)
            if step + 2 < steps:
                yield from low_chain(step + 2)

    def second():
        for step in range(0, steps, 2):
            yield from down_chain(step)
            if step + 1 < steps:
                yield from low_chain(step + 1)
                yield from up_chain(step + 1)
            if step + 2 < steps:
                yield from lift_chain(step + 2)

    together([gather(0, 0, 2)])
    for load in loads[3:]:
        load.wait()
    both = project(0, 0, 2)
    state["low", 0], state["lift", 0] = both[:rank], both[rank:]
    together([first(), second()], ORDER)
    a_end, b_end = state["a", steps], state["b", steps]

    fa_ref[...] = a_end
    fb_ref[...] = b_end
    left = jnp.concatenate([a_end, -a_now], axis=0).T
    right = jnp.concatenate([b_end, b_now], axis=0)
    change = branch_scale * exact(left, right, ((1,), (0,)))
    nb_ref[...] = base_ref[...] + change if add_base else change
    for copy in sent:
        copy.wait_send()


def local(inputs, targets, base, adapter_a, adapter_b):
    n = lax.axis_size("fsdp")
    workers = lax.axis_size("worker")
    nz = n // 8
    tokens, wanted, a, b = inputs[0], targets[0], adapter_a[0], adapter_b[0].T
    steps, rows, width = tokens.shape
    rank, shard = a.shape
    features = b.shape[1]
    whole = base
    if workers > 1:
        whole = lax.all_gather(base.astype(bf16), "worker", axis=1, tiled=True).astype(f32)
    vmem = pl.BlockSpec(memory_space=pltpu.VMEM)
    block = (rank, shard)
    cut = (rank // 8, features)
    nzs = max(nz - 1, 1)
    per_gather = (nz - 1) + 3 * nz + 4
    messages = (2 * steps - 1) * per_gather + 2 * steps * (7 + nz - 1) + steps * (14 + nz - 1)
    merged, final_a, final_b = pl.pallas_call(
        functools.partial(kernel, nz, workers == 1),
        out_shape=(
            jax.ShapeDtypeStruct((shard, features), f32),
            jax.ShapeDtypeStruct(block, f32),
            jax.ShapeDtypeStruct((rank, features), f32),
        ),
        in_specs=[pl.BlockSpec(memory_space=pl.ANY)] * 5,
        out_specs=(vmem, vmem, vmem),
        scratch_shapes=[
            pltpu.VMEM((steps, rows, width), bf16),
            pltpu.VMEM(wanted.shape, bf16),
            pltpu.VMEM((shard, features), f32),
            pltpu.VMEM(block, f32),
            pltpu.VMEM((rank, features), f32),
            pltpu.VMEM((steps, 2, 4, nz, 2) + block, bf16),
            pltpu.VMEM((2, 4, nz) + block, f32),
            pltpu.VMEM((steps, 2, 4, nz) + block, bf16),
            pltpu.VMEM((steps, 2, 4, nz) + block, bf16),
            pltpu.VMEM((steps, 2, 3, nz) + block, bf16),
            pltpu.VMEM((steps, 2, 3, nz) + block, bf16),
            pltpu.VMEM((steps, 2, nzs) + block, bf16),
            pltpu.VMEM((steps, 2, nzs) + block, bf16),
            pltpu.VMEM((steps, 8) + cut, f32),
            pltpu.VMEM((steps, 7) + cut, f32),
            pltpu.VMEM((steps, nz) + cut, f32),
            pltpu.VMEM((steps, 8) + cut, f32),
            pltpu.SemaphoreType.DMA((messages,)),
            pltpu.SemaphoreType.DMA((messages,)),
            pltpu.SemaphoreType.DMA((steps + 4,)),
        ],
        compiler_params=pltpu.CompilerParams(
            collective_id=0, has_side_effects=True, vmem_limit_bytes=60 * 1024 * 1024
        ),
    )(tokens, wanted, whole, a, b)
    if workers > 1:
        share = lax.psum_scatter(merged, "worker", scatter_dimension=1, tiled=True)
        merged = base + share / workers
    return (merged, final_a[None], final_b.T[None])


def solution(mesh):
    return jax.shard_map(
        local,
        mesh=mesh,
        in_specs=(
            P("worker", None, "fsdp", None),
            P("worker", None, "fsdp", None),
            P("fsdp", "worker"),
            P("worker", None, "fsdp"),
            P("worker", None, None),
        ),
        out_specs=(P("fsdp", "worker"), P("worker", None, "fsdp"), P("worker", None, None)),
        check_vma=False,
    )
```
